512 devices in a mesh: dp: 16 (over y_hi, x, core), tm: 8 (over z), height: 4 (over y_lo).
Axes of the slice: x: 4, y: 8 (y_hi: 2, y_lo: 4; y = y_hi * 4 + y_lo), z: 8, core: 2. Of those that a mesh axis runs over, the one named last changes fastest.
Arguments:
- probe_vectors: bfloat16 [16, 48, 32, 3, 1536], P('dp', 'tm', 'height'), may hold values from -24 to 24
- lookup_vectors: bfloat16 [16, 48, 32, 3, 1536], P('dp', 'tm', 'height'), may hold values from -24 to 24
- payload_vectors: bfloat16 [16, 48, 32, 3, 1536], P('dp', 'tm', 'height'), may hold values from -4.5 to 4.5
- result_derivative: bfloat16 [16, 48, 32, 3, 1536], P('dp', 'tm', 'height'), may hold values from -48 to 48
- patch_occupancy: int32 [16, 8, 4], P('dp'), may hold values from 63 to 144, as said below
- patch_neighborhood_offset: int32 [16, 8, 4, 2], P('dp'), may hold values from -1 to 1
- sharpness: float32 [12], replicated, may hold values from 0.7 to 1.4
Outputs:
- probe_derivative: bfloat16 [16, 48, 32, 3, 1536], P('dp', 'tm', 'height')
- lookup_derivative: bfloat16 [16, 48, 32, 3, 1536], P('dp', 'tm', 'height')
- payload_derivative: bfloat16 [16, 48, 32, 3, 1536], P('dp', 'tm', 'height')
- sharpness_derivative: float32 [12], replicated
The draws below stay inside these ranges and needn't reach their ends.
Inputs may be any that keep to these rules, and one draw needn't show every extreme that they name: `patch_occupancy`: valid slots are the first ones of a tile in slot order; every tile off the last time tile and the last height tile is full.
All inputs are finite; a program needn't handle non-finite values.
Results may differ from the reference program's by a relative error of at most 0.022.
Values may be sent and summed in bfloat16 or wider, within the bound.
No kernel may reach another device: no remote copies, remote signals or barrier semaphores. Data moves between devices by JAX's collectives and lax.ppermute only.
A program may use at most 128 MiB of HBM per device.

```python
import math
import jax
import jax.numpy as jnp
from jax import lax

FOCUS_BRANCHES = 12
HEAD_DIM = 128
WIDTH = 1536
TILE_T = 6
TILE_H = 8
COLS = 3
TILE_LEN = 144
TIME_TILES = 8
HIGH_TILES = 4
FRAMES = 48
ROWS = 32
CLIPS = 16


def out_of_tiles(tiled):
    shaped = tiled.reshape(CLIPS, TIME_TILES, HIGH_TILES, TILE_T, TILE_H, COLS, WIDTH)
    shaped = jnp.transpose(shaped, (0, 1, 3, 2, 4, 5, 6))
    return shaped.reshape(CLIPS, FRAMES, ROWS, COLS, WIDTH)


def drawn_normal(key):
    return jnp.clip(jax.random.normal(key, (CLIPS, TIME_TILES, HIGH_TILES, TILE_LEN, WIDTH), jnp.float32), -4.5, 4.5)


def draw_probe_vectors(key, part):
    key = jax.random.fold_in(key, 5)
    values = drawn_normal(key)
    return out_of_tiles(values).astype(jnp.bfloat16)


def draw_lookup_vectors(key, part):
    key = jax.random.fold_in(key, 7)
    values = drawn_normal(key)
    return out_of_tiles(values).astype(jnp.bfloat16)


def draw_result_derivative(key, part):
    key = jax.random.fold_in(key, 9)
    array_shape = (CLIPS, FRAMES, ROWS, COLS, WIDTH)
    clip_pos = jnp.arange(CLIPS, dtype=jnp.float32)[:, None, None, None, None]
    frame_pos = jnp.arange(FRAMES, dtype=jnp.float32)[None, :, None, None, None]
    row_pos = jnp.arange(ROWS, dtype=jnp.float32)[None, None, :, None, None]
    order = (clip_pos * FRAMES + frame_pos) * ROWS + row_pos
    ramp = order / max(CLIPS * FRAMES * ROWS - 1, 1)
    values = jnp.clip(jax.random.normal(key, array_shape, jnp.float32), -4.5, 4.5) * jnp.power(3.0, ramp)
    return values.astype(jnp.bfloat16)


def draw_patch_occupancy(key, part):
    key = jax.random.fold_in(key, 13)
    spacing = TILE_LEN // 16
    cuts = jax.random.randint(key, (CLIPS, TIME_TILES, HIGH_TILES), 0, 10)
    time_ids = jnp.arange(TIME_TILES, dtype=jnp.int32)[None, :, None]
    high_ids = jnp.arange(HIGH_TILES, dtype=jnp.int32)[None, None, :]
    border = (time_ids == TIME_TILES - 1) | (high_ids == HIGH_TILES - 1)
    counts = jnp.where(border, TILE_LEN - spacing * cuts, TILE_LEN).astype(jnp.int32)
    counts = counts.at[:, TIME_TILES - 1, HIGH_TILES - 1].set(TILE_LEN - 9 * spacing)
    return counts.astype(jnp.int32)


def draw_patch_neighborhood_offset(key, part):
    key = jax.random.fold_in(key, 17)
    shifts = jax.random.randint(key, (CLIPS, TIME_TILES, HIGH_TILES, 2), -1, 2)
    shifts = shifts.at[:, 0, 0, 0].set(-1)
    shifts = shifts.at[:, 0, 0, 1].set(1)
    return shifts.astype(jnp.int32)


def steps_of(own_key, dims, split, least, largest):
    def one(dim, parts):
        heights = jax.random.uniform(jax.random.fold_in(jax.random.fold_in(own_key, 6), dim), (parts,), jnp.float32, least / len(split), largest / len(split))
        return jnp.repeat(jnp.exp(heights), dims[dim] // parts).reshape((-1,) + (1,) * (len(dims) - dim - 1))

    factor_of = one(*split[0])
    for cut in split[1:]:
        factor_of = factor_of * one(*cut)
    return factor_of


def normal_values(own_key, extent, scale, limit, split=(), kind=jnp.bfloat16):
    entries = jax.random.normal(own_key, extent, jnp.float32) * scale
    if len(split) > 0:
        entries = steps_of(own_key, extent, split, -0.22, 0.18) * entries
    return jnp.clip(entries, min=-limit, max=limit).astype(kind)


def setup_inputs(seed: int = 0) -> dict:
    seeds = jax.random.split(jax.random.key(seed), 8)
    probe_vectors = draw_probe_vectors(jax.random.fold_in(seeds[7], 71), 0)
    lookup_vectors = draw_lookup_vectors(jax.random.fold_in(seeds[7], 71), 0)
    payload_vectors = normal_values(seeds[2], (CLIPS, FRAMES, ROWS, COLS, WIDTH), 1.0, 4.5, ((0, 16), (1, 8), (2, 4)))
    result_derivative = draw_result_derivative(jax.random.fold_in(seeds[7], 71), 0)
    patch_occupancy = draw_patch_occupancy(jax.random.fold_in(seeds[7], 71), 0)
    patch_neighborhood_offset = draw_patch_neighborhood_offset(jax.random.fold_in(seeds[7], 71), 0)
    sharpness = jnp.clip(jnp.exp(jax.random.uniform(seeds[6], (FOCUS_BRANCHES,), jnp.float32, math.log(0.7), math.log(1.4))), 0.7, 1.4)
    return dict(probe_vectors=probe_vectors, lookup_vectors=lookup_vectors, payload_vectors=payload_vectors, result_derivative=result_derivative, patch_occupancy=patch_occupancy, patch_neighborhood_offset=patch_neighborhood_offset, sharpness=sharpness)


def to_tiles(field):
    feature_width = field.shape[-1]
    shaped = field.reshape(TIME_TILES, TILE_T, HIGH_TILES, TILE_H, COLS, feature_width)
    shaped = jnp.transpose(shaped, (0, 2, 1, 3, 4, 5))
    return shaped.reshape(TIME_TILES, HIGH_TILES, TILE_LEN, feature_width)

def from_tiles(tiled):
    feature_width = tiled.shape[-1]
    shaped = tiled.reshape(TIME_TILES, HIGH_TILES, TILE_T, TILE_H, COLS, feature_width)
    shaped = jnp.transpose(shaped, (0, 2, 1, 3, 4, 5))
    return shaped.reshape(FRAMES, ROWS, COLS, feature_width)

def padded_tiles(tiled):
    return jnp.pad(tiled.astype(jnp.float32), ((1, 1), (1, 1), (0, 0), (0, 0)))

def video_derivatives(probe_vectors, lookup_vectors, payload_vectors, result_derivative, patch_occupancy, patch_neighborhood_offset, sharpness):
    reciprocal_radical = 1.0 / math.sqrt(HEAD_DIM)
    query_pad = padded_tiles(to_tiles(probe_vectors))
    key_pad = padded_tiles(to_tiles(lookup_vectors))
    value_pad = padded_tiles(to_tiles(payload_vectors))
    grad_pad = padded_tiles(to_tiles(result_derivative))
    count_pad = jnp.pad(patch_occupancy, 1)
    shift_pad = jnp.pad(patch_neighborhood_offset, ((1, 1), (1, 1), (0, 0)))
    token_slot = jnp.arange(TILE_LEN, dtype=jnp.int32)
    relative = jnp.arange(3, dtype=jnp.int32) - 1
    rel_time = jnp.repeat(relative, 3)
    rel_high = jnp.tile(relative, 3)
    zero = jnp.zeros((), jnp.int32)
    sharpness_numbers = sharpness.astype(jnp.float32)
    sharpness_vertical = sharpness_numbers[:, None, None, None]
    derivative_multiplier = (sharpness_numbers * reciprocal_radical)[:, None, None, None]

    def own_block(table, time_tile, high_tile):
        block = lax.dynamic_slice(table, (time_tile + 1, high_tile + 1, zero, zero), (1, 1) + table.shape[2:])
        return block.reshape(TILE_LEN, FOCUS_BRANCHES, -1)

    def near_block(table, time_tile, high_tile):
        block = lax.dynamic_slice(table, (time_tile, high_tile, zero, zero), (3, 3) + table.shape[2:])
        return block.reshape(9, TILE_LEN, FOCUS_BRANCHES, -1)

    def query_side(tile_id):
        time_tile = tile_id // HIGH_TILES
        high_tile = tile_id % HIGH_TILES
        query = own_block(query_pad, time_tile, high_tile)
        grad = own_block(grad_pad, time_tile, high_tile)
        near_keys = near_block(key_pad, time_tile, high_tile)
        near_values = near_block(value_pad, time_tile, high_tile)
        counts_near = lax.dynamic_slice(count_pad, (time_tile, high_tile), (3, 3)).reshape(9)
        own_shift = lax.dynamic_slice(shift_pad, (time_tile + 1, high_tile + 1, zero), (1, 1, 2)).reshape(2)
        inside = (jnp.abs(rel_time - own_shift[0]) <= 1) & (jnp.abs(rel_high - own_shift[1]) <= 1)
        key_allowed = (token_slot[None, :] < counts_near[:, None]) & inside[:, None]
        query_valid = token_slot < counts_near[4]
        unscaled_logit = jnp.einsum('qhd,nkhd->hqnk', query, near_keys) * reciprocal_radical
        logits_table = sharpness_vertical * unscaled_logit
        allowed = key_allowed[None, None]
        masked = jnp.where(allowed, logits_table, -jnp.inf)
        row_max = lax.optimization_barrier(jnp.max(masked, axis=(2, 3)))
        log_total = row_max + jnp.log(lax.optimization_barrier(jnp.sum(jnp.exp(masked - row_max[:, :, None, None]), axis=(2, 3))))
        permitted_mask = allowed & query_valid[None, :, None, None]
        probabilities = jnp.where(permitted_mask, jnp.exp(logits_table - log_total[:, :, None, None]), 0.0)
        rounded = lax.optimization_barrier(probabilities.astype(jnp.bfloat16)).astype(jnp.float32)
        attended = jnp.einsum('hqnk,nkhd->qhd', rounded, near_values)
        row_delta = lax.optimization_barrier(jnp.sum(grad * attended, axis=2))
        grad_weight = jnp.einsum('qhd,nkhd->hqnk', grad, near_values)
        logit_derivative = probabilities * (grad_weight - row_delta.T[:, :, None, None])
        scaled = lax.optimization_barrier((logit_derivative * derivative_multiplier).astype(jnp.bfloat16)).astype(jnp.float32)
        grad_q = jnp.einsum('hqnk,nkhd->qhd', scaled, near_keys).reshape(TILE_LEN, WIDTH)
        grad_temp = lax.optimization_barrier(jnp.sum(logit_derivative * unscaled_logit, axis=(1, 2, 3)))
        return (grad_q, log_total.T, row_delta, grad_temp)
    tile_ids = jnp.arange(TIME_TILES * HIGH_TILES, dtype=jnp.int32)
    grad_q, log_total, row_delta, grad_temp = lax.map(query_side, tile_ids)
    total_pad = padded_tiles(log_total.reshape(TIME_TILES, HIGH_TILES, TILE_LEN, FOCUS_BRANCHES))
    delta_pad = padded_tiles(row_delta.reshape(TIME_TILES, HIGH_TILES, TILE_LEN, FOCUS_BRANCHES))

    def key_side(tile_id):
        time_tile = tile_id // HIGH_TILES
        high_tile = tile_id % HIGH_TILES
        key = own_block(key_pad, time_tile, high_tile)
        value = own_block(value_pad, time_tile, high_tile)
        near_queries = near_block(query_pad, time_tile, high_tile)
        near_grads = near_block(grad_pad, time_tile, high_tile)
        near_total = near_block(total_pad, time_tile, high_tile)[..., 0]
        near_delta = near_block(delta_pad, time_tile, high_tile)[..., 0]
        counts_near = lax.dynamic_slice(count_pad, (time_tile, high_tile), (3, 3)).reshape(9)
        shifts_near = lax.dynamic_slice(shift_pad, (time_tile, high_tile, zero), (3, 3, 2)).reshape(9, 2)
        inside = (jnp.abs(-rel_time - shifts_near[:, 0]) <= 1) & (jnp.abs(-rel_high - shifts_near[:, 1]) <= 1)
        query_ok = token_slot[None, :] < counts_near[:, None]
        key_ok = token_slot < counts_near[4]
        permitted_mask = inside[:, None, None] & query_ok[:, :, None] & key_ok[None, None, :]
        unscaled_logit = jnp.einsum('nqhd,khd->hnqk', near_queries, key) * reciprocal_radical
        normalizers = jnp.transpose(near_total, (2, 0, 1))[:, :, :, None]
        probabilities = jnp.where(permitted_mask[None], jnp.exp(sharpness_vertical * unscaled_logit - normalizers), 0.0)
        rounded = lax.optimization_barrier(probabilities.astype(jnp.bfloat16)).astype(jnp.float32)
        grad_weight = jnp.einsum('nqhd,khd->hnqk', near_grads, value)
        deltas = jnp.transpose(near_delta, (2, 0, 1))[:, :, :, None]
        logit_derivative = probabilities * (grad_weight - deltas)
        scaled = lax.optimization_barrier((logit_derivative * derivative_multiplier).astype(jnp.bfloat16)).astype(jnp.float32)
        part_k = jnp.einsum('hnqk,nqhd->nkhd', scaled, near_queries)
        part_v = jnp.einsum('hnqk,nqhd->nkhd', rounded, near_grads)
        part_k = lax.optimization_barrier(part_k.astype(jnp.bfloat16)).astype(jnp.float32)
        part_v = lax.optimization_barrier(part_v.astype(jnp.bfloat16)).astype(jnp.float32)
        grad_k = lax.optimization_barrier(jnp.sum(part_k, axis=0)).reshape(TILE_LEN, WIDTH)
        grad_v = lax.optimization_barrier(jnp.sum(part_v, axis=0)).reshape(TILE_LEN, WIDTH)
        return (grad_k, grad_v)
    grad_k, grad_v = lax.map(key_side, tile_ids)
    shape_tiles = (TIME_TILES, HIGH_TILES, TILE_LEN, WIDTH)
    probe_derivative = from_tiles(grad_q.reshape(shape_tiles)).astype(jnp.bfloat16)
    lookup_derivative = from_tiles(grad_k.reshape(shape_tiles)).astype(jnp.bfloat16)
    payload_derivative = from_tiles(grad_v.reshape(shape_tiles)).astype(jnp.bfloat16)
    return (probe_derivative, lookup_derivative, payload_derivative, lax.optimization_barrier(jnp.sum(grad_temp, axis=0)))

def reference(probe_vectors, lookup_vectors, payload_vectors, result_derivative, patch_occupancy, patch_neighborhood_offset, sharpness):

    def per_clip(element_sequence):
        return video_derivatives(element_sequence[0], element_sequence[1], element_sequence[2], element_sequence[3], element_sequence[4], element_sequence[5], sharpness)
    probe_derivative, lookup_derivative, payload_derivative, grad_temp = lax.map(per_clip, (probe_vectors, lookup_vectors, payload_vectors, result_derivative, patch_occupancy, patch_neighborhood_offset))
    return (probe_derivative, lookup_derivative, payload_derivative, lax.optimization_barrier(jnp.sum(grad_temp, axis=0)))
```

```python
import functools
import math

import jax
import jax.numpy as jnp
import numpy as np
from jax import lax
from jax.experimental import pallas as pl
from jax.experimental.pallas import tpu as pltpu
from jax.sharding import PartitionSpec as P

ALL_AXES = ("dp", "tm", "height")
HIDDEN = -1e30


def shifted(block, axis, step):
    count = lax.axis_size(axis)
    pairs = [(i, i + step) for i in range(count) if 0 <= i + step < count]
    return lax.ppermute(block, axis, pairs)


def gathered_everywhere(row):
    count = math.prod(lax.axis_size(axis) for axis in ALL_AXES)
    sent = jnp.broadcast_to(row[None], (count,) + row.shape)
    return lax.all_to_all(sent, ALL_AXES, 0, 0)


def sum_body(rows_ref, own_ref, below_ref, above_ref, row_ref, own_sum_ref, *side_refs):
    row_ref[...] = jnp.sum(rows_ref[...], axis=0)
    length = own_sum_ref.shape[0]
    for n in range(3):
        rows = slice(n * length, (n + 1) * length)
        summed = (
            own_ref[rows].astype(jnp.float32)
            + below_ref[rows].astype(jnp.float32)
            + above_ref[rows].astype(jnp.float32)
        )
        if n == 0:
            own_sum_ref[...] = summed
        else:
            side_refs[n - 1][...] = summed.astype(jnp.bfloat16)


def summed_parts(rows, own, below, above):
    tile = (own.shape[0] // 3, own.shape[1])
    vmem = pl.BlockSpec(memory_space=pltpu.VMEM)
    return pl.pallas_call(
        sum_body,
        in_specs=[vmem] * 4,
        out_specs=[vmem] * 4,
        out_shape=[
            jax.ShapeDtypeStruct(rows.shape[1:], jnp.float32),
            jax.ShapeDtypeStruct(tile, jnp.float32),
            jax.ShapeDtypeStruct(tile, jnp.bfloat16),
            jax.ShapeDtypeStruct(tile, jnp.bfloat16),
        ],
        compiler_params=pltpu.CompilerParams(vmem_limit_bytes=16 * 1024 * 1024),
    )(rows, own, below, above)


LINE = (0, -1, 1)
KEY_TILES = [(a, b) for b in LINE for a in LINE]
VALUE_SPOTS = [(LINE.index(a), LINE.index(b)) for a, b in KEY_TILES]


def raw_scores(query, grad, keys, values, logits_ref, grad_weight_ref):
    across = (((1,), (1,)), ((), ()))
    logits_ref[...] = lax.dot_general(query, keys, across, preferred_element_type=jnp.float32)
    grad_weight_ref[...] = lax.dot_general(
        grad, values, across, preferred_element_type=jnp.float32
    )


def score_gradients(multiplier, bias_ref, valid_ref, logits_ref, grad_weight_ref, low_ref, scaled_ref):
    rows_at_once = 16
    for first in range(0, logits_ref.shape[0], rows_at_once):
        rows = slice(first, first + rows_at_once)
        logits = logits_ref[rows] * multiplier + bias_ref[...]
        raised = jnp.exp2(logits - jnp.max(logits, axis=1, keepdims=True))
        total = jnp.sum(raised, axis=1, keepdims=True)
        weights = raised * (valid_ref[rows] / total)
        low = weights.astype(jnp.bfloat16)
        low_ref[rows] = low
        grad_weight = grad_weight_ref[rows]
        row_delta = jnp.sum(low.astype(jnp.float32) * grad_weight, axis=1, keepdims=True)
        scaled_ref[rows] = (weights * (grad_weight - row_delta)).astype(jnp.bfloat16)


def attention_body(
    opening,
    tile_len,
    together,
    kept,
    sharpness_ref,
    counts_ref,
    shifts_ref,
    slot_row_ref,
    slot_col_ref,
    query_ref,
    grad_ref,
    *refs,
):
    key_refs, value_refs = refs[:3], refs[3:6]
    refs = refs[6 + kept :]
    query_grad_ref, sharpness_grad_ref = refs[0], refs[1]
    key_part_refs, value_part_refs = refs[2:5], refs[5:8]
    bias_ref, valid_ref = refs[8], refs[9]
    work = [refs[10 + 4 * j : 14 + 4 * j] for j in range(together)]
    head_dim = query_ref.shape[1] // together
    time_tile = lax.axis_index("tm")
    high_tile = lax.axis_index("height")
    high_count, time_count = counts_ref.shape[0], counts_ref.shape[1]
    time_shift = shifts_ref[2 * high_tile, time_tile]
    high_shift = shifts_ref[2 * high_tile + 1, time_tile]

    @pl.when(pl.program_id(0) == 0)
    def _():
        limits = []
        for dt, dh in KEY_TILES:
            t, h = time_tile + dt, high_tile + dh
            inside = (t >= 0) & (t < time_count) & (h >= 0) & (h < high_count)
            inside &= (jnp.abs(dt - time_shift) <= 1) & (jnp.abs(dh - high_shift) <= 1)
            count = counts_ref[jnp.clip(h, 0, high_count - 1), jnp.clip(t, 0, time_count - 1)]
            limits.append(jnp.where(inside, count, 0))
        place = lax.broadcasted_iota(jnp.int32, slot_row_ref.shape, 1)
        limit_row = jnp.full(slot_row_ref.shape, limits[0], jnp.int32)
        for n in range(1, len(limits)):
            limit_row = jnp.where(place >= n * tile_len, limits[n], limit_row)
        bias_ref[...] = jnp.where(slot_row_ref[...] < limit_row, 0.0, HIDDEN)
        own_count = counts_ref[high_tile, time_tile]
        valid_ref[...] = jnp.where(slot_col_ref[...] < own_count, 1.0, 0.0)

    def tile(ref, n):
        return ref[n * tile_len : (n + 1) * tile_len]

    def operands(j):
        columns = slice(j * head_dim, (j + 1) * head_dim)
        keys = jnp.concatenate([ref[:, columns] for ref in key_refs], axis=0)
        values = jnp.concatenate(
            [tile(value_refs[b], n)[:, columns] for b, n in VALUE_SPOTS], axis=0
        )
        return query_ref[:, columns], grad_ref[:, columns], keys, values

    def gradients(j):
        columns = slice(j * head_dim, (j + 1) * head_dim)
        query, grad, keys, values = operands(j)
        sharp = sharpness_ref[opening + pl.program_id(0) * together + j]
        factor = sharp * (1.0 / math.sqrt(head_dim))
        logits_ref, grad_weight_ref, low_ref, scaled_ref = work[j]
        score_gradients(factor * math.log2(math.e), bias_ref, valid_ref, *work[j])
        low, scaled = low_ref[...], scaled_ref[...]
        down = (((0,), (0,)), ((), ()))
        query_grad = jnp.dot(scaled, keys, preferred_element_type=jnp.float32) * factor
        query_grad_ref[:, columns] = query_grad.astype(jnp.bfloat16)
        sharpness_grad_ref[j] = jnp.sum(
            query_grad * query.astype(jnp.float32), axis=0, keepdims=True
        ) * (1.0 / sharp)
        part_key = lax.dot_general(scaled, query, down, preferred_element_type=jnp.float32)
        part_key = (part_key * factor).astype(jnp.bfloat16)
        part_value = lax.dot_general(low, grad, down, preferred_element_type=jnp.float32)
        part_value = part_value.astype(jnp.bfloat16)
        for n, ref in enumerate(key_part_refs):
            ref[:, columns] = part_key[3 * n * tile_len : 3 * (n + 1) * tile_len]
        for place, (b, n) in enumerate(VALUE_SPOTS):
            value_part_refs[b][n * tile_len : (n + 1) * tile_len, columns] = tile(
                part_value, place
            )

    raw_scores(*operands(0), *work[0][:2])
    for j in range(together):
        if j + 1 < together:
            raw_scores(*operands(j + 1), *work[j + 1][:2])
        gradients(j)


def attention(chunk, branches, tile_len, head_dim, small, query, grad, keys, values, so_far):
    opening, heads = chunk
    together = 2
    first = opening // together
    smem = pl.BlockSpec(memory_space=pltpu.SMEM)
    whole = lambda array: pl.BlockSpec(array.shape, lambda h: (0, 0))
    side = pl.BlockSpec((tile_len, together * head_dim), lambda h: (0, first + h))
    near = pl.BlockSpec((3 * tile_len, together * head_dim), lambda h: (0, h))
    out_near = pl.BlockSpec((3 * tile_len, together * head_dim), lambda h: (0, first + h))
    part = jax.ShapeDtypeStruct((3 * tile_len, branches * head_dim), jnp.bfloat16)
    pairs = heads * tile_len * 9 * tile_len
    score = (tile_len, 9 * tile_len)
    return pl.pallas_call(
        functools.partial(attention_body, opening, tile_len, together, len(so_far)),
        grid=(heads // together,),
        in_specs=[smem] * 3
        + [whole(small[3]), whole(small[4]), side, side]
        + [near] * 6
        + [pl.BlockSpec(memory_space=pl.ANY)] * len(so_far),
        out_specs=[side, pl.BlockSpec((together, 1, head_dim), lambda h: (first + h, 0, 0))]
        + [out_near] * 6,
        out_shape=[
            jax.ShapeDtypeStruct((tile_len, branches * head_dim), jnp.bfloat16),
            jax.ShapeDtypeStruct((branches, 1, head_dim), jnp.float32),
        ]
        + [part] * 6,
        input_output_aliases={13 + n: n for n in range(len(so_far))},
        scratch_shapes=[
            pltpu.VMEM((1, 9 * tile_len), jnp.float32),
            pltpu.VMEM((tile_len, 1), jnp.float32),
        ]
        + [
            pltpu.VMEM(score, jnp.float32),
            pltpu.VMEM(score, jnp.float32),
            pltpu.VMEM(score, jnp.bfloat16),
            pltpu.VMEM(score, jnp.bfloat16),
        ]
        * together,
        compiler_params=pltpu.CompilerParams(vmem_limit_bytes=16 * 1024 * 1024),
        cost_estimate=pl.CostEstimate(
            flops=10 * pairs * head_dim,
            bytes_accessed=12 * 3 * tile_len * heads * head_dim * 2,
            transcendentals=pairs,
        ),
    )(*small, query, grad, *keys, *values, *so_far)


def pack_body(chunks, *refs):
    inputs, outputs = refs[:3], refs[3:]
    tile_len = inputs[0].shape[0]
    head_dim = inputs[0].shape[1] // sum(heads for _, heads in chunks)
    for (opening, heads), out_ref in zip(chunks, outputs):
        columns = slice(opening * head_dim, (opening + heads) * head_dim)
        for n in range(3):
            out_ref[n * tile_len : (n + 1) * tile_len] = inputs[n][:, columns]


def packed(chunks, line):
    tile_len, width = line[0].shape
    per_head = width // sum(heads for _, heads in chunks)
    vmem = pl.BlockSpec(memory_space=pltpu.VMEM)
    return pl.pallas_call(
        functools.partial(pack_body, chunks),
        in_specs=[vmem] * 3,
        out_specs=[vmem] * len(chunks),
        out_shape=[
            jax.ShapeDtypeStruct((3 * tile_len, heads * per_head), jnp.bfloat16)
            for _, heads in chunks
        ],
        compiler_params=pltpu.CompilerParams(vmem_limit_bytes=8 * 1024 * 1024),
    )(*line)


def on_device(
    probe_vectors,
    lookup_vectors,
    payload_vectors,
    result_derivative,
    patch_occupancy,
    patch_neighborhood_offset,
    sharpness,
):
    _, frames, rows, cols, width = probe_vectors.shape
    tile_len = frames * rows * cols
    branches = sharpness.shape[0]
    head_dim = width // branches

    def as_tokens(field):
        return jnp.transpose(field[0], (0, 2, 1, 3)).reshape(tile_len, width)

    def as_field(tokens):
        return jnp.transpose(tokens.reshape(frames, cols, rows, width), (0, 2, 1, 3))[None]

    spot = np.arange(tile_len)
    slot = (spot // (cols * rows) * rows + spot % rows) * cols + spot // rows % cols
    slot_row = jnp.asarray(np.tile(slot, 9)[None, :], jnp.int32)
    slot_col = jnp.asarray(slot[:, None], jnp.int32)
    counts = patch_occupancy[0].T
    shifts = jnp.transpose(patch_neighborhood_offset[0], (1, 2, 0)).reshape(-1, counts.shape[1])
    small = (sharpness, counts, shifts, slot_row, slot_col)

    query, key, value, grad = (
        as_tokens(f) for f in (probe_vectors, lookup_vectors, payload_vectors, result_derivative)
    )
    chunks = ((0, 6), (6, 6))
    key_blocks = packed(chunks, (key, shifted(key, "tm", 1), shifted(key, "tm", -1)))
    value_blocks = packed(
        chunks, (value, shifted(value, "height", 1), shifted(value, "height", -1))
    )
    near = [
        (
            (keys, shifted(keys, "height", 1), shifted(keys, "height", -1)),
            (values, shifted(values, "tm", 1), shifted(values, "tm", -1)),
        )
        for keys, values in zip(key_blocks, value_blocks)
    ]
    results = ()
    for chunk, (keys, values) in zip(chunks, near):
        results = attention(
            chunk, branches, tile_len, head_dim, small, query, grad, keys, values, results
        )
    query_grad, sharpness_grad = results[0], results[1]

    def met(parts, second):
        own, below, above = parts
        return own, shifted(below, second, -1), shifted(above, second, 1)

    def completed(own, below, above, first):
        return (
            own
            + shifted(below, first, -1).astype(jnp.float32)
            + shifted(above, first, 1).astype(jnp.float32)
        ).astype(jnp.bfloat16)

    key_parts = met(results[2:5], "height")
    value_parts = met(results[5:8], "tm")
    row = jnp.sum(sharpness_grad, axis=(1, 2))
    all_rows = gathered_everywhere(jnp.pad(row, (0, -branches % 128))[None])
    summed = sum(part.astype(jnp.float32) for part in key_parts)
    key_grad = completed(
        summed[:tile_len],
        summed[tile_len : 2 * tile_len].astype(jnp.bfloat16),
        summed[2 * tile_len :].astype(jnp.bfloat16),
        "tm",
    )
    row, *summed = summed_parts(all_rows, *value_parts)
    value_grad = completed(*summed, "height")
    return as_field(query_grad), as_field(key_grad), as_field(value_grad), row[0, :branches]


def solution(mesh):
    field = P("dp", "tm", "height", None, None)
    return jax.shard_map(
        on_device,
        mesh=mesh,
        in_specs=(field,) * 4 + (P("dp", None, None), P("dp", None, None, None), P()),
        out_specs=(field,) * 3 + (P(),),
        check_vma=False,
    )
```

```python
import functools
import math

import jax
import jax.numpy as jnp
import numpy as np
from jax import lax
from jax.experimental import pallas as pl
from jax.experimental.pallas import tpu as pltpu
from jax.sharding import PartitionSpec as P

HIDDEN = -1e30


def exchanged(block, axis, turn):
    count = lax.axis_size(axis)
    partner = [(i + turn) // 2 * 4 + 1 - 2 * turn - i for i in range(count)]
    return lax.ppermute(block, axis, [(i, j) for i, j in enumerate(partner) if 0 <= j < count])


def gathered(row, axes):
    count = math.prod(lax.axis_size(axis) for axis in axes)
    sent = jnp.broadcast_to(row[None], (count,) + row.shape)
    return lax.all_to_all(sent, axes, 0, 0)


def sum_body(with_rows, *refs):
    if with_rows:
        rows_ref, row_ref = refs[0], refs[4]
        row_ref[...] = jnp.sum(rows_ref[...], axis=0)
        refs = refs[1:4] + refs[5:]
    own_ref, below_ref, above_ref, own_sum_ref, *side_refs = refs
    length = own_sum_ref.shape[0]
    for n in range(3):
        rows = slice(n * length, (n + 1) * length)
        summed = (
            own_ref[rows].astype(jnp.float32)
            + below_ref[rows].astype(jnp.float32)
            + above_ref[rows].astype(jnp.float32)
        )
        if n == 0:
            own_sum_ref[...] = summed
        else:
            side_refs[n - 1][...] = summed.astype(jnp.bfloat16)


def summed_parts(parts, rows=None):
    tile = (parts[0].shape[0] // 3, parts[0].shape[1])
    vmem = pl.BlockSpec(memory_space=pltpu.VMEM)
    given = (() if rows is None else (rows,)) + tuple(parts)
    out_shape = [
        jax.ShapeDtypeStruct(tile, jnp.float32),
        jax.ShapeDtypeStruct(tile, jnp.bfloat16),
        jax.ShapeDtypeStruct(tile, jnp.bfloat16),
    ]
    if rows is not None:
        out_shape = [jax.ShapeDtypeStruct(rows.shape[1:], jnp.float32)] + out_shape
    return pl.pallas_call(
        functools.partial(sum_body, rows is not None),
        in_specs=[vmem] * len(given),
        out_specs=[vmem] * len(out_shape),
        out_shape=out_shape,
        compiler_params=pltpu.CompilerParams(vmem_limit_bytes=16 * 1024 * 1024),
    )(*given)


def final_body(with_rows, *refs):
    if with_rows:
        rows_ref, row_ref = refs[0], refs[4]
        row_ref[...] = jnp.sum(rows_ref[...], axis=0)
        refs = refs[1:4] + refs[5:]
    own_ref, below_ref, above_ref, out_ref = refs
    out_ref[...] = (
        own_ref[...] + below_ref[...].astype(jnp.float32) + above_ref[...].astype(jnp.float32)
    ).astype(out_ref.dtype)


def final_sum(parts, rows=None):
    vmem = pl.BlockSpec(memory_space=pltpu.VMEM)
    given = (() if rows is None else (rows,)) + tuple(parts)
    out_shape = [jax.ShapeDtypeStruct(parts[0].shape, jnp.bfloat16)]
    if rows is not None:
        out_shape = [jax.ShapeDtypeStruct(rows.shape[1:], jnp.float32)] + out_shape
    return pl.pallas_call(
        functools.partial(final_body, rows is not None),
        in_specs=[vmem] * len(given),
        out_specs=[vmem] * len(out_shape),
        out_shape=out_shape,
        compiler_params=pltpu.CompilerParams(vmem_limit_bytes=8 * 1024 * 1024),
    )(*given)


KEY_SPOTS = [(a, b) for a in range(3) for b in range(3)]
VALUE_SPOTS = [(b, a) for a, b in KEY_SPOTS]


def line(place):
    first = 1 - 2 * (place % 2)
    return place, place + first, place - first


def raw_scores(query, grad, keys, values, logits_ref, grad_weight_ref):
    across = (((1,), (1,)), ((), ()))
    logits_ref[...] = lax.dot_general(query, keys, across, preferred_element_type=jnp.float32)
    grad_weight_ref[...] = lax.dot_general(
        grad, values, across, preferred_element_type=jnp.float32
    )


def score_gradients(multiplier, bias_ref, valid_ref, logits_ref, grad_weight_ref, low_ref, scaled_ref):
    rows_at_once = 16
    for first in range(0, logits_ref.shape[0], rows_at_once):
        rows = slice(first, first + rows_at_once)
        logits = logits_ref[rows] * multiplier + bias_ref[...]
        raised = jnp.exp2(logits - jnp.max(logits, axis=1, keepdims=True))
        total = jnp.sum(raised, axis=1, keepdims=True)
        weights = raised * (valid_ref[rows] / total)
        low = weights.astype(jnp.bfloat16)
        low_ref[rows] = low
        grad_weight = grad_weight_ref[rows]
        row_delta = jnp.sum(low.astype(jnp.float32) * grad_weight, axis=1, keepdims=True)
        scaled_ref[rows] = (weights * (grad_weight - row_delta)).astype(jnp.bfloat16)


def attention_body(
    opening,
    tile_len,
    together,
    kept,
    sharpness_ref,
    counts_ref,
    shifts_ref,
    slot_row_ref,
    slot_col_ref,
    query_ref,
    grad_ref,
    *refs,
):
    key_refs, value_refs = refs[:3], refs[3:6]
    refs = refs[6 + kept :]
    query_grad_ref, sharpness_grad_ref = refs[0], refs[1]
    key_part_refs, value_part_refs = refs[2:5], refs[5:8]
    bias_ref, valid_ref = refs[8], refs[9]
    work = [refs[10 + 4 * j : 14 + 4 * j] for j in range(together)]
    head_dim = query_ref.shape[1] // together
    time_tile = lax.axis_index("tm")
    high_tile = lax.axis_index("height")
    high_count, time_count = counts_ref.shape[0], counts_ref.shape[1]
    time_shift = shifts_ref[2 * high_tile, time_tile]
    high_shift = shifts_ref[2 * high_tile + 1, time_tile]

    @pl.when(pl.program_id(0) == 0)
    def _():
        limits = []
        times, highs = line(time_tile), line(high_tile)
        for a, b in KEY_SPOTS:
            t, h = times[b], highs[a]
            inside = (t >= 0) & (t < time_count) & (h >= 0) & (h < high_count)
            inside &= jnp.abs(t - time_tile - time_shift) <= 1
            inside &= jnp.abs(h - high_tile - high_shift) <= 1
            count = counts_ref[jnp.clip(h, 0, high_count - 1), jnp.clip(t, 0, time_count - 1)]
            limits.append(jnp.where(inside, count, 0))
        place = lax.broadcasted_iota(jnp.int32, slot_row_ref.shape, 1)
        limit_row = jnp.full(slot_row_ref.shape, limits[0], jnp.int32)
        for n in range(1, len(limits)):
            limit_row = jnp.where(place >= n * tile_len, limits[n], limit_row)
        bias_ref[...] = jnp.where(slot_row_ref[...] < limit_row, 0.0, HIDDEN)
        own_count = counts_ref[high_tile, time_tile]
        valid_ref[...] = jnp.where(slot_col_ref[...] < own_count, 1.0, 0.0)

    def tile(ref, n):
        return ref[n * tile_len : (n + 1) * tile_len]

    def operands(j):
        columns = slice(j * head_dim, (j + 1) * head_dim)
        place = (pl.program_id(0) * together + j) * head_dim
        near = pl.ds(pl.multiple_of(place, head_dim), head_dim)
        keys = jnp.concatenate([ref[:, near] for ref in key_refs], axis=0)
        values = jnp.concatenate(
            [value_refs[b][n * tile_len : (n + 1) * tile_len, near] for b, n in VALUE_SPOTS],
            axis=0,
        )
        return query_ref[:, columns], grad_ref[:, columns], keys, values

    def gradients(j):
        columns = slice(j * head_dim, (j + 1) * head_dim)
        query, grad, keys, values = operands(j)
        sharp = sharpness_ref[opening + pl.program_id(0) * together + j]
        factor = sharp * (1.0 / math.sqrt(head_dim))
        logits_ref, grad_weight_ref, low_ref, scaled_ref = work[j]
        score_gradients(factor * math.log2(math.e), bias_ref, valid_ref, *work[j])
        low, scaled = low_ref[...], scaled_ref[...]
        down = (((0,), (0,)), ((), ()))
        query_grad = jnp.dot(scaled, keys, preferred_element_type=jnp.float32) * factor
        query_grad_ref[:, columns] = query_grad.astype(jnp.bfloat16)
        sharpness_grad_ref[j] = jnp.sum(
            query_grad * query.astype(jnp.float32), axis=0, keepdims=True
        ) * (1.0 / sharp)
        part_key = lax.dot_general(scaled, query, down, preferred_element_type=jnp.float32)
        part_key = (part_key * factor).astype(jnp.bfloat16)
        part_value = lax.dot_general(low, grad, down, preferred_element_type=jnp.float32)
        part_value = part_value.astype(jnp.bfloat16)
        for n, ref in enumerate(key_part_refs):
            ref[:, columns] = part_key[3 * n * tile_len : 3 * (n + 1) * tile_len]
        for place, (b, n) in enumerate(VALUE_SPOTS):
            value_part_refs[b][n * tile_len : (n + 1) * tile_len, columns] = tile(
                part_value, place
            )

    raw_scores(*operands(0), *work[0][:2])
    for j in range(together):
        if j + 1 < together:
            raw_scores(*operands(j + 1), *work[j + 1][:2])
        gradients(j)


def attention(chunk, branches, tile_len, head_dim, small, query, grad, keys, values, so_far):
    opening, heads = chunk
    together = 2
    first = opening // together
    smem = pl.BlockSpec(memory_space=pltpu.SMEM)
    whole = lambda array: pl.BlockSpec(array.shape, lambda h: (0, 0))
    side = pl.BlockSpec((tile_len, together * head_dim), lambda h: (0, first + h))
    out_near = pl.BlockSpec((3 * tile_len, together * head_dim), lambda h: (0, first + h))
    part = jax.ShapeDtypeStruct((3 * tile_len, branches * head_dim), jnp.bfloat16)
    pairs = heads * tile_len * 9 * tile_len
    score = (tile_len, 9 * tile_len)
    return pl.pallas_call(
        functools.partial(attention_body, opening, tile_len, together, len(so_far)),
        grid=(heads // together,),
        in_specs=[smem] * 3
        + [whole(small[3]), whole(small[4]), side, side]
        + [pl.BlockSpec(memory_space=pltpu.VMEM)] * 6
        + [pl.BlockSpec(memory_space=pl.ANY)] * len(so_far),
        out_specs=[side, pl.BlockSpec((together, 1, head_dim), lambda h: (first + h, 0, 0))]
        + [out_near] * 6,
        out_shape=[
            jax.ShapeDtypeStruct((tile_len, branches * head_dim), jnp.bfloat16),
            jax.ShapeDtypeStruct((branches, 1, head_dim), jnp.float32),
        ]
        + [part] * 6,
        input_output_aliases={13 + n: n for n in range(len(so_far))},
        scratch_shapes=[
            pltpu.VMEM((1, 9 * tile_len), jnp.float32),
            pltpu.VMEM((tile_len, 1), jnp.float32),
        ]
        + [
            pltpu.VMEM(score, jnp.float32),
            pltpu.VMEM(score, jnp.float32),
            pltpu.VMEM(score, jnp.bfloat16),
            pltpu.VMEM(score, jnp.bfloat16),
        ]
        * together,
        compiler_params=pltpu.CompilerParams(vmem_limit_bytes=24 * 1024 * 1024),
        cost_estimate=pl.CostEstimate(
            flops=10 * pairs * head_dim,
            bytes_accessed=12 * 3 * tile_len * heads * head_dim * 2,
            transcendentals=pairs,
        ),
    )(*small, query, grad, *keys, *values, *so_far)


def pack_body(chunks, *refs):
    inputs, outputs = refs[:3], refs[3:]
    tile_len = inputs[0].shape[0]
    head_dim = inputs[0].shape[1] // sum(heads for _, heads in chunks)
    for (opening, heads), out_ref in zip(chunks, outputs):
        columns = slice(opening * head_dim, (opening + heads) * head_dim)
        for n in range(3):
            out_ref[n * tile_len : (n + 1) * tile_len] = inputs[n][:, columns]


def packed(chunks, line):
    tile_len, width = line[0].shape
    per_head = width // sum(heads for _, heads in chunks)
    vmem = pl.BlockSpec(memory_space=pltpu.VMEM)
    return pl.pallas_call(
        functools.partial(pack_body, chunks),
        in_specs=[vmem] * 3,
        out_specs=[vmem] * len(chunks),
        out_shape=[
            jax.ShapeDtypeStruct((3 * tile_len, heads * per_head), jnp.bfloat16)
            for _, heads in chunks
        ],
        compiler_params=pltpu.CompilerParams(vmem_limit_bytes=8 * 1024 * 1024),
    )(*line)


def on_device(
    probe_vectors,
    lookup_vectors,
    payload_vectors,
    result_derivative,
    patch_occupancy,
    patch_neighborhood_offset,
    sharpness,
):
    _, frames, high, cols, width = probe_vectors.shape
    tile_len = frames * high * cols
    branches = sharpness.shape[0]
    head_dim = width // branches

    def as_tokens(field):
        return jnp.transpose(field[0], (0, 2, 1, 3)).reshape(tile_len, width)

    def as_field(tokens):
        return jnp.transpose(tokens.reshape(frames, cols, high, width), (0, 2, 1, 3))[None]

    spot = np.arange(tile_len)
    slot = (spot // (cols * high) * high + spot % high) * cols + spot // high % cols
    slot_row = jnp.asarray(np.tile(slot, 9)[None, :], jnp.int32)
    slot_col = jnp.asarray(slot[:, None], jnp.int32)
    counts = patch_occupancy[0].T
    shifts = jnp.transpose(patch_neighborhood_offset[0], (1, 2, 0)).reshape(-1, counts.shape[1])
    small = (sharpness, counts, shifts, slot_row, slot_col)

    query, key, value, grad = (
        as_tokens(f) for f in (probe_vectors, lookup_vectors, payload_vectors, result_derivative)
    )
    chunks = ((0, 6), (6, 6))
    key_blocks = packed(chunks, (key, exchanged(key, "tm", 0), exchanged(key, "tm", 1)))
    value_blocks = packed(
        chunks, (value, exchanged(value, "height", 0), exchanged(value, "height", 1))
    )
    near = [
        (
            (keys, exchanged(keys, "height", 0), exchanged(keys, "height", 1)),
            (values, exchanged(values, "tm", 0), exchanged(values, "tm", 1)),
        )
        for keys, values in zip(key_blocks, value_blocks)
    ]
    results = ()
    for chunk, (keys, values) in zip(chunks, near):
        results = attention(
            chunk, branches, tile_len, head_dim, small, query, grad, keys, values, results
        )
    query_grad, sharpness_grad = results[0], results[1]

    def met(parts, axis):
        return parts[0], exchanged(parts[1], axis, 0), exchanged(parts[2], axis, 1)

    key_parts = met(results[2:5], "height")
    value_parts = met(results[5:8], "tm")
    row = jnp.sum(sharpness_grad, axis=(1, 2))[None]
    row, *summed = summed_parts(key_parts, gathered(row, ("dp",)))
    (key_grad,) = final_sum(met(summed, "tm"))
    row, *summed = summed_parts(value_parts, row[None])
    rows = gathered(row, ("tm", "height"))
    row, value_grad = final_sum(met(summed, "height"), rows)
    return as_field(query_grad), as_field(key_grad), as_field(value_grad), row[0]


def solution(mesh):
    field = P("dp", "tm", "height", None, None)
    return jax.shard_map(
        on_device,
        mesh=mesh,
        in_specs=(field,) * 4 + (P("dp", None, None), P("dp", None, None, None), P()),
        out_specs=(field,) * 3 + (P(),),
        check_vma=False,
    )
```

```python
import functools
import math

import jax
import jax.numpy as jnp
import numpy as np
from jax import lax
from jax.experimental import pallas as pl
from jax.experimental.pallas import tpu as pltpu
from jax.sharding import PartitionSpec as P

HIDDEN = -1e30


def exchanged(block, axis, turn):
    count = lax.axis_size(axis)
    partner = [(i + turn) // 2 * 4 + 1 - 2 * turn - i for i in range(count)]
    return lax.ppermute(block, axis, [(i, j) for i, j in enumerate(partner) if 0 <= j < count])


def swapped(rows, axes):
    return lax.all_to_all(rows, axes, 0, 0)


def sum_body(with_rows, *refs):
    if with_rows:
        rows_ref, row_ref = refs[0], refs[4]
        row_ref[...] = jnp.broadcast_to(jnp.sum(rows_ref[...], axis=0)[None], row_ref.shape)
        refs = refs[1:4] + refs[5:]
    own_ref, below_ref, above_ref, own_sum_ref, *side_refs = refs
    length = own_sum_ref.shape[0]
    for n in range(3):
        rows = slice(n * length, (n + 1) * length)
        summed = (
            own_ref[rows].astype(jnp.float32)
            + below_ref[rows].astype(jnp.float32)
            + above_ref[rows].astype(jnp.float32)
        )
        if n == 0:
            own_sum_ref[...] = summed
        else:
            side_refs[n - 1][...] = summed.astype(jnp.bfloat16)


def summed_parts(parts, rows=None, copies=1):
    tile = (parts[0].shape[0] // 3, parts[0].shape[1])
    vmem = pl.BlockSpec(memory_space=pltpu.VMEM)
    given = (() if rows is None else (rows,)) + tuple(parts)
    out_shape = [
        jax.ShapeDtypeStruct(tile, jnp.float32),
        jax.ShapeDtypeStruct(tile, jnp.bfloat16),
        jax.ShapeDtypeStruct(tile, jnp.bfloat16),
    ]
    if rows is not None:
        out_shape = [jax.ShapeDtypeStruct((copies,) + rows.shape[1:], jnp.float32)] + out_shape
    return pl.pallas_call(
        functools.partial(sum_body, rows is not None),
        in_specs=[vmem] * len(given),
        out_specs=[vmem] * len(out_shape),
        out_shape=out_shape,
        compiler_params=pltpu.CompilerParams(vmem_limit_bytes=16 * 1024 * 1024),
    )(*given)


def final_body(with_rows, *refs):
    if with_rows:
        rows_ref, row_ref = refs[0], refs[4]
        row_ref[...] = jnp.sum(rows_ref[...], axis=0)
        refs = refs[1:4] + refs[5:]
    own_ref, below_ref, above_ref, out_ref = refs
    out_ref[...] = (
        own_ref[...] + below_ref[...].astype(jnp.float32) + above_ref[...].astype(jnp.float32)
    ).astype(out_ref.dtype)


def final_sum(parts, rows=None):
    vmem = pl.BlockSpec(memory_space=pltpu.VMEM)
    given = (() if rows is None else (rows,)) + tuple(parts)
    out_shape = [jax.ShapeDtypeStruct(parts[0].shape, jnp.bfloat16)]
    if rows is not None:
        out_shape = [jax.ShapeDtypeStruct(rows.shape[1:], jnp.float32)] + out_shape
    return pl.pallas_call(
        functools.partial(final_body, rows is not None),
        in_specs=[vmem] * len(given),
        out_specs=[vmem] * len(out_shape),
        out_shape=out_shape,
        compiler_params=pltpu.CompilerParams(vmem_limit_bytes=8 * 1024 * 1024),
    )(*given)


KEY_SPOTS = [(a, b) for a in range(3) for b in range(3)]
VALUE_SPOTS = [(b, a) for a, b in KEY_SPOTS]


def line(place):
    first = 1 - 2 * (place % 2)
    return place, place + first, place - first


def raw_scores(query, grad, keys, values, logits_ref, grad_weight_ref):
    across = (((1,), (1,)), ((), ()))
    logits_ref[...] = lax.dot_general(query, keys, across, preferred_element_type=jnp.float32)
    grad_weight_ref[...] = lax.dot_general(
        grad, values, across, preferred_element_type=jnp.float32
    )


def score_gradients(multiplier, bias_ref, valid_ref, logits_ref, grad_weight_ref, low_ref, scaled_ref):
    rows_at_once = 16
    for first in range(0, logits_ref.shape[0], rows_at_once):
        rows = slice(first, first + rows_at_once)
        logits = logits_ref[rows] * multiplier + bias_ref[...]
        raised = jnp.exp2(logits - jnp.max(logits, axis=1, keepdims=True))
        total = jnp.sum(raised, axis=1, keepdims=True)
        weights = raised * (valid_ref[rows] / total)
        low = weights.astype(jnp.bfloat16)
        low_ref[rows] = low
        grad_weight = grad_weight_ref[rows]
        row_delta = jnp.sum(low.astype(jnp.float32) * grad_weight, axis=1, keepdims=True)
        scaled_ref[rows] = (weights * (grad_weight - row_delta)).astype(jnp.bfloat16)


def attention_body(
    opening,
    tile_len,
    together,
    kept,
    sharpness_ref,
    counts_ref,
    shifts_ref,
    slot_row_ref,
    slot_col_ref,
    query_ref,
    grad_ref,
    *refs,
):
    key_refs, value_refs = refs[:3], refs[3:6]
    refs = refs[6 + kept :]
    query_grad_ref, sharpness_grad_ref = refs[0], refs[1]
    key_part_refs, value_part_refs = refs[2:5], refs[5:8]
    bias_ref, valid_ref = refs[8], refs[9]
    work = [refs[10 + 4 * j : 14 + 4 * j] for j in range(together)]
    head_dim = query_ref.shape[1] // together
    time_tile = lax.axis_index("tm")
    high_tile = lax.axis_index("height")
    high_count, time_count = counts_ref.shape[0], counts_ref.shape[1]
    time_shift = shifts_ref[2 * high_tile, time_tile]
    high_shift = shifts_ref[2 * high_tile + 1, time_tile]

    @pl.when(pl.program_id(0) == 0)
    def _():
        limits = []
        times, highs = line(time_tile), line(high_tile)
        for a, b in KEY_SPOTS:
            t, h = times[b], highs[a]
            inside = (t >= 0) & (t < time_count) & (h >= 0) & (h < high_count)
            inside &= jnp.abs(t - time_tile - time_shift) <= 1
            inside &= jnp.abs(h - high_tile - high_shift) <= 1
            count = counts_ref[jnp.clip(h, 0, high_count - 1), jnp.clip(t, 0, time_count - 1)]
            limits.append(jnp.where(inside, count, 0))
        place = lax.broadcasted_iota(jnp.int32, slot_row_ref.shape, 1)
        limit_row = jnp.full(slot_row_ref.shape, limits[0], jnp.int32)
        for n in range(1, len(limits)):
            limit_row = jnp.where(place >= n * tile_len, limits[n], limit_row)
        bias_ref[...] = jnp.where(slot_row_ref[...] < limit_row, 0.0, HIDDEN)
        own_count = counts_ref[high_tile, time_tile]
        valid_ref[...] = jnp.where(slot_col_ref[...] < own_count, 1.0, 0.0)

    def tile(ref, n):
        return ref[n * tile_len : (n + 1) * tile_len]

    def operands(j):
        columns = slice(j * head_dim, (j + 1) * head_dim)
        place = (pl.program_id(0) * together + j) * head_dim
        near = pl.ds(pl.multiple_of(place, head_dim), head_dim)
        keys = jnp.concatenate([ref[:, near] for ref in key_refs], axis=0)
        values = jnp.concatenate(
            [value_refs[b][n * tile_len : (n + 1) * tile_len, near] for b, n in VALUE_SPOTS],
            axis=0,
        )
        return query_ref[:, columns], grad_ref[:, columns], keys, values

    def gradients(j):
        columns = slice(j * head_dim, (j + 1) * head_dim)
        query, grad, keys, values = operands(j)
        sharp = sharpness_ref[opening + pl.program_id(0) * together + j]
        factor = sharp * (1.0 / math.sqrt(head_dim))
        logits_ref, grad_weight_ref, low_ref, scaled_ref = work[j]
        score_gradients(factor * math.log2(math.e), bias_ref, valid_ref, *work[j])
        low, scaled = low_ref[...], scaled_ref[...]
        down = (((0,), (0,)), ((), ()))
        query_grad = jnp.dot(scaled, keys, preferred_element_type=jnp.float32) * factor
        query_grad_ref[:, columns] = query_grad.astype(jnp.bfloat16)
        sharpness_grad_ref[j] = jnp.sum(
            query_grad * query.astype(jnp.float32), axis=0, keepdims=True
        ) * (1.0 / sharp)
        part_key = lax.dot_general(scaled, query, down, preferred_element_type=jnp.float32)
        part_key = (part_key * factor).astype(jnp.bfloat16)
        part_value = lax.dot_general(low, grad, down, preferred_element_type=jnp.float32)
        part_value = part_value.astype(jnp.bfloat16)
        for n, ref in enumerate(key_part_refs):
            ref[:, columns] = part_key[3 * n * tile_len : 3 * (n + 1) * tile_len]
        for place, (b, n) in enumerate(VALUE_SPOTS):
            value_part_refs[b][n * tile_len : (n + 1) * tile_len, columns] = tile(
                part_value, place
            )

    raw_scores(*operands(0), *work[0][:2])
    for j in range(together):
        if j + 1 < together:
            raw_scores(*operands(j + 1), *work[j + 1][:2])
        gradients(j)


def attention(chunk, branches, tile_len, head_dim, small, query, grad, keys, values, so_far):
    opening, heads = chunk
    together = 2
    first = opening // together
    smem = pl.BlockSpec(memory_space=pltpu.SMEM)
    whole = lambda array: pl.BlockSpec(array.shape, lambda h: (0, 0))
    side = pl.BlockSpec((tile_len, together * head_dim), lambda h: (0, first + h))
    out_near = pl.BlockSpec((3 * tile_len, together * head_dim), lambda h: (0, first + h))
    part = jax.ShapeDtypeStruct((3 * tile_len, branches * head_dim), jnp.bfloat16)
    pairs = heads * tile_len * 9 * tile_len
    score = (tile_len, 9 * tile_len)
    return pl.pallas_call(
        functools.partial(attention_body, opening, tile_len, together, len(so_far)),
        grid=(heads // together,),
        in_specs=[smem] * 3
        + [whole(small[3]), whole(small[4]), side, side]
        + [pl.BlockSpec(memory_space=pltpu.VMEM)] * 6
        + [pl.BlockSpec(memory_space=pl.ANY)] * len(so_far),
        out_specs=[side, pl.BlockSpec((together, 1, head_dim), lambda h: (first + h, 0, 0))]
        + [out_near] * 6,
        out_shape=[
            jax.ShapeDtypeStruct((tile_len, branches * head_dim), jnp.bfloat16),
            jax.ShapeDtypeStruct((branches, 1, head_dim), jnp.float32),
        ]
        + [part] * 6,
        input_output_aliases={13 + n: n for n in range(len(so_far))},
        scratch_shapes=[
            pltpu.VMEM((1, 9 * tile_len), jnp.float32),
            pltpu.VMEM((tile_len, 1), jnp.float32),
        ]
        + [
            pltpu.VMEM(score, jnp.float32),
            pltpu.VMEM(score, jnp.float32),
            pltpu.VMEM(score, jnp.bfloat16),
            pltpu.VMEM(score, jnp.bfloat16),
        ]
        * together,
        compiler_params=pltpu.CompilerParams(vmem_limit_bytes=24 * 1024 * 1024),
        cost_estimate=pl.CostEstimate(
            flops=10 * pairs * head_dim,
            bytes_accessed=12 * 3 * tile_len * heads * head_dim * 2,
            transcendentals=pairs,
        ),
    )(*small, query, grad, *keys, *values, *so_far)


def pack_body(chunks, *refs):
    inputs, outputs = refs[:3], refs[3:]
    tile_len = inputs[0].shape[0]
    head_dim = inputs[0].shape[1] // sum(heads for _, heads in chunks)
    for (opening, heads), out_ref in zip(chunks, outputs):
        columns = slice(opening * head_dim, (opening + heads) * head_dim)
        for n in range(3):
            out_ref[n * tile_len : (n + 1) * tile_len] = inputs[n][:, columns]


def own_body(own_ref, out_ref):
    out_ref[...] = own_ref[...]


def packed(chunks, line):
    tile_len, width = line[0].shape
    whole = pl.BlockSpec(memory_space=pltpu.VMEM)
    own = pl.pallas_call(
        own_body,
        in_specs=[whole],
        out_specs=whole,
        out_shape=jax.ShapeDtypeStruct(line[0].shape, line[0].dtype),
        compiler_params=pltpu.CompilerParams(vmem_limit_bytes=8 * 1024 * 1024),
    )(line[0])
    line = (own,) + line[1:]
    per_head = width // sum(heads for _, heads in chunks)
    return pl.pallas_call(
        functools.partial(pack_body, chunks),
        in_specs=[whole] * 3,
        out_specs=[whole] * len(chunks),
        out_shape=[
            jax.ShapeDtypeStruct((3 * tile_len, heads * per_head), jnp.bfloat16)
            for _, heads in chunks
        ],
        compiler_params=pltpu.CompilerParams(vmem_limit_bytes=8 * 1024 * 1024),
    )(*line)


def on_device(
    probe_vectors,
    lookup_vectors,
    payload_vectors,
    result_derivative,
    patch_occupancy,
    patch_neighborhood_offset,
    sharpness,
):
    _, frames, high, cols, width = probe_vectors.shape
    tile_len = frames * high * cols
    branches = sharpness.shape[0]
    head_dim = width // branches

    def as_tokens(field):
        return jnp.transpose(field[0], (0, 2, 1, 3)).reshape(tile_len, width)

    def as_field(tokens):
        return jnp.transpose(tokens.reshape(frames, cols, high, width), (0, 2, 1, 3))[None]

    spot = np.arange(tile_len)
    slot = (spot // (cols * high) * high + spot % high) * cols + spot // high % cols
    slot_row = jnp.asarray(np.tile(slot, 9)[None, :], jnp.int32)
    slot_col = jnp.asarray(slot[:, None], jnp.int32)
    counts = patch_occupancy[0].T
    shifts = jnp.transpose(patch_neighborhood_offset[0], (1, 2, 0)).reshape(-1, counts.shape[1])
    small = (sharpness, counts, shifts, slot_row, slot_col)

    query, key, value, grad = (
        as_tokens(f) for f in (probe_vectors, lookup_vectors, payload_vectors, result_derivative)
    )
    chunks = ((0, 6), (6, 6))
    key_blocks = packed(chunks, (key, exchanged(key, "tm", 0), exchanged(key, "tm", 1)))
    value_blocks = packed(
        chunks, (value, exchanged(value, "height", 0), exchanged(value, "height", 1))
    )
    near = [
        (
            (keys, exchanged(keys, "height", 0), exchanged(keys, "height", 1)),
            (values, exchanged(values, "tm", 0), exchanged(values, "tm", 1)),
        )
        for keys, values in zip(key_blocks, value_blocks)
    ]
    results = ()
    for chunk, (keys, values) in zip(chunks, near):
        results = attention(
            chunk, branches, tile_len, head_dim, small, query, grad, keys, values, results
        )
    query_grad, sharpness_grad = results[0], results[1]

    def met(parts, axis):
        return parts[0], exchanged(parts[1], axis, 0), exchanged(parts[2], axis, 1)

    key_parts = met(results[2:5], "height")
    value_parts = met(results[5:8], "tm")
    wide, time_count = ("dp", "height"), lax.axis_size("tm")
    row = jnp.sum(sharpness_grad, axis=(1, 2))
    rows = jnp.broadcast_to(row, (math.prod(lax.axis_size(axis) for axis in wide), 1, branches))
    row, *summed = summed_parts(key_parts, swapped(rows, wide))
    (key_grad,) = final_sum(met(summed, "tm"))
    rows, *summed = summed_parts(value_parts, row, time_count)
    rows = swapped(rows, ("tm",))
    row, value_grad = final_sum(met(summed, "height"), rows)
    return as_field(query_grad), as_field(key_grad), as_field(value_grad), row[0]


def solution(mesh):
    field = P("dp", "tm", "height", None, None)
    return jax.shard_map(
        on_device,
        mesh=mesh,
        in_specs=(field,) * 4 + (P("dp", None, None), P("dp", None, None, None), P()),
        out_specs=(field,) * 3 + (P(),),
        check_vma=False,
    )
```

```python
import functools
import math

import jax
import jax.numpy as jnp
import numpy as np
from jax import lax
from jax.experimental import pallas as pl
from jax.experimental.pallas import tpu as pltpu
from jax.sharding import PartitionSpec as P

HIDDEN = -1e30


def exchanged(block, axis, turn):
    count = lax.axis_size(axis)
    partner = [(i + turn) // 2 * 4 + 1 - 2 * turn - i for i in range(count)]
    return lax.ppermute(block, axis, [(i, j) for i, j in enumerate(partner) if 0 <= j < count])


def swapped(rows, axes):
    return lax.all_to_all(rows, axes, 0, 0)


def sum_body(with_rows, *refs):
    if with_rows:
        rows_ref, row_ref = refs[0], refs[4]
        row_ref[...] = jnp.broadcast_to(jnp.sum(rows_ref[...], axis=0)[None], row_ref.shape)
        refs = refs[1:4] + refs[5:]
    own_ref, below_ref, above_ref, own_sum_ref, *side_refs = refs
    length = own_sum_ref.shape[0]
    for n in range(3):
        rows = slice(n * length, (n + 1) * length)
        summed = (
            own_ref[rows].astype(jnp.float32)
            + below_ref[rows].astype(jnp.float32)
            + above_ref[rows].astype(jnp.float32)
        )
        if n == 0:
            own_sum_ref[...] = summed
        else:
            side_refs[n - 1][...] = summed.astype(jnp.bfloat16)


def summed_parts(parts, rows=None, copies=1):
    tile = (parts[0].shape[0] // 3, parts[0].shape[1])
    vmem = pl.BlockSpec(memory_space=pltpu.VMEM)
    given = (() if rows is None else (rows,)) + tuple(parts)
    out_shape = [
        jax.ShapeDtypeStruct(tile, jnp.float32),
        jax.ShapeDtypeStruct(tile, jnp.bfloat16),
        jax.ShapeDtypeStruct(tile, jnp.bfloat16),
    ]
    if rows is not None:
        out_shape = [jax.ShapeDtypeStruct((copies,) + rows.shape[1:], jnp.float32)] + out_shape
    return pl.pallas_call(
        functools.partial(sum_body, rows is not None),
        in_specs=[vmem] * len(given),
        out_specs=[vmem] * len(out_shape),
        out_shape=out_shape,
        compiler_params=pltpu.CompilerParams(vmem_limit_bytes=16 * 1024 * 1024),
    )(*given)


def final_body(with_rows, *refs):
    if with_rows:
        rows_ref, row_ref = refs[0], refs[4]
        row_ref[...] = jnp.sum(rows_ref[...], axis=0)
        refs = refs[1:4] + refs[5:]
    own_ref, below_ref, above_ref, out_ref = refs
    out_ref[...] = (
        own_ref[...] + below_ref[...].astype(jnp.float32) + above_ref[...].astype(jnp.float32)
    ).astype(out_ref.dtype)


def final_sum(parts, rows=None):
    vmem = pl.BlockSpec(memory_space=pltpu.VMEM)
    given = (() if rows is None else (rows,)) + tuple(parts)
    out_shape = [jax.ShapeDtypeStruct(parts[0].shape, jnp.bfloat16)]
    if rows is not None:
        out_shape = [jax.ShapeDtypeStruct(rows.shape[1:], jnp.float32)] + out_shape
    return pl.pallas_call(
        functools.partial(final_body, rows is not None),
        in_specs=[vmem] * len(given),
        out_specs=[vmem] * len(out_shape),
        out_shape=out_shape,
        compiler_params=pltpu.CompilerParams(vmem_limit_bytes=8 * 1024 * 1024),
    )(*given)


KEY_SPOTS = [(a, b) for a in range(3) for b in range(3)]
VALUE_SPOTS = [(b, a) for a, b in KEY_SPOTS]


def line(place):
    first = 1 - 2 * (place % 2)
    return place, place + first, place - first


def raw_scores(query, grad, keys, values, logits_ref, grad_weight_ref):
    across = (((1,), (1,)), ((), ()))
    logits_ref[...] = lax.dot_general(query, keys, across, preferred_element_type=jnp.float32)
    grad_weight_ref[...] = lax.dot_general(
        grad, values, across, preferred_element_type=jnp.float32
    )


def score_gradients(multiplier, bias_ref, valid_ref, logits_ref, grad_weight_ref, low_ref, scaled_ref):
    rows_at_once = 16
    for first in range(0, logits_ref.shape[0], rows_at_once):
        rows = slice(first, first + rows_at_once)
        logits = logits_ref[rows] * multiplier + bias_ref[...]
        raised = jnp.exp2(logits - jnp.max(logits, axis=1, keepdims=True))
        total = jnp.sum(raised, axis=1, keepdims=True)
        weights = raised * (valid_ref[rows] / total)
        low = weights.astype(jnp.bfloat16)
        low_ref[rows] = low
        grad_weight = grad_weight_ref[rows]
        row_delta = jnp.sum(low.astype(jnp.float32) * grad_weight, axis=1, keepdims=True)
        scaled_ref[rows] = (weights * (grad_weight - row_delta)).astype(jnp.bfloat16)


def attention_body(
    opening,
    tile_len,
    together,
    kept,
    sharpness_ref,
    counts_ref,
    shifts_ref,
    slot_row_ref,
    slot_col_ref,
    query_ref,
    grad_ref,
    *refs,
):
    key_refs, value_refs = refs[:3], refs[3:6]
    refs = refs[6 + kept :]
    query_grad_ref, sharpness_grad_ref = refs[0], refs[1]
    key_part_refs, value_part_refs = refs[2:5], refs[5:8]
    bias_ref, valid_ref = refs[8], refs[9]
    work = (refs[10:14], refs[14:18])
    head_dim = query_ref.shape[1] // together
    time_tile = lax.axis_index("tm")
    high_tile = lax.axis_index("height")
    high_count, time_count = counts_ref.shape[0], counts_ref.shape[1]
    time_shift = shifts_ref[2 * high_tile, time_tile]
    high_shift = shifts_ref[2 * high_tile + 1, time_tile]

    @pl.when(pl.program_id(0) == 0)
    def _():
        limits = []
        times, highs = line(time_tile), line(high_tile)
        for a, b in KEY_SPOTS:
            t, h = times[b], highs[a]
            inside = (t >= 0) & (t < time_count) & (h >= 0) & (h < high_count)
            inside &= jnp.abs(t - time_tile - time_shift) <= 1
            inside &= jnp.abs(h - high_tile - high_shift) <= 1
            count = counts_ref[jnp.clip(h, 0, high_count - 1), jnp.clip(t, 0, time_count - 1)]
            limits.append(jnp.where(inside, count, 0))
        place = lax.broadcasted_iota(jnp.int32, slot_row_ref.shape, 1)
        limit_row = jnp.full(slot_row_ref.shape, limits[0], jnp.int32)
        for n in range(1, len(limits)):
            limit_row = jnp.where(place >= n * tile_len, limits[n], limit_row)
        bias_ref[...] = jnp.where(slot_row_ref[...] < limit_row, 0.0, HIDDEN)
        own_count = counts_ref[high_tile, time_tile]
        valid_ref[...] = jnp.where(slot_col_ref[...] < own_count, 1.0, 0.0)

    def tile(ref, n):
        return ref[n * tile_len : (n + 1) * tile_len]

    def operands(j):
        columns = slice(j * head_dim, (j + 1) * head_dim)
        place = (pl.program_id(0) * together + j) * head_dim
        near = pl.ds(pl.multiple_of(place, head_dim), head_dim)
        keys = jnp.concatenate([ref[:, near] for ref in key_refs], axis=0)
        values = jnp.concatenate(
            [value_refs[b][n * tile_len : (n + 1) * tile_len, near] for b, n in VALUE_SPOTS],
            axis=0,
        )
        return query_ref[:, columns], grad_ref[:, columns], keys, values

    def gradients(j):
        columns = slice(j * head_dim, (j + 1) * head_dim)
        query, grad, keys, values = operands(j)
        sharp = sharpness_ref[opening + pl.program_id(0) * together + j]
        factor = sharp * (1.0 / math.sqrt(head_dim))
        logits_ref, grad_weight_ref, low_ref, scaled_ref = work[j % 2]
        score_gradients(factor * math.log2(math.e), bias_ref, valid_ref, *work[j % 2])
        low, scaled = low_ref[...], scaled_ref[...]
        down = (((0,), (0,)), ((), ()))
        query_grad = jnp.dot(scaled, keys, preferred_element_type=jnp.float32) * factor
        query_grad_ref[:, columns] = query_grad.astype(jnp.bfloat16)
        sharpness_grad_ref[j] = jnp.sum(
            query_grad * query.astype(jnp.float32), axis=0, keepdims=True
        ) * (1.0 / sharp)
        part_key = lax.dot_general(scaled, query, down, preferred_element_type=jnp.float32)
        part_key = (part_key * factor).astype(jnp.bfloat16)
        part_value = lax.dot_general(low, grad, down, preferred_element_type=jnp.float32)
        part_value = part_value.astype(jnp.bfloat16)
        for n, ref in enumerate(key_part_refs):
            ref[:, columns] = part_key[3 * n * tile_len : 3 * (n + 1) * tile_len]
        for place, (b, n) in enumerate(VALUE_SPOTS):
            value_part_refs[b][n * tile_len : (n + 1) * tile_len, columns] = tile(
                part_value, place
            )

    raw_scores(*operands(0), *work[0][:2])
    for j in range(together):
        if j + 1 < together:
            raw_scores(*operands(j + 1), *work[(j + 1) % 2][:2])
        gradients(j)


def attention(chunk, branches, tile_len, head_dim, small, query, grad, keys, values, so_far):
    opening, heads = chunk
    together = heads
    first = opening // together
    smem = pl.BlockSpec(memory_space=pltpu.SMEM)
    whole = lambda array: pl.BlockSpec(array.shape, lambda h: (0, 0))
    side = pl.BlockSpec((tile_len, together * head_dim), lambda h: (0, first + h))
    out_near = pl.BlockSpec((3 * tile_len, together * head_dim), lambda h: (0, first + h))
    part = jax.ShapeDtypeStruct((3 * tile_len, branches * head_dim), jnp.bfloat16)
    pairs = heads * tile_len * 9 * tile_len
    score = (tile_len, 9 * tile_len)
    return pl.pallas_call(
        functools.partial(attention_body, opening, tile_len, together, len(so_far)),
        grid=(heads // together,),
        in_specs=[smem] * 3
        + [whole(small[3]), whole(small[4]), side, side]
        + [pl.BlockSpec(memory_space=pltpu.VMEM)] * 6
        + [pl.BlockSpec(memory_space=pl.ANY)] * len(so_far),
        out_specs=[side, pl.BlockSpec((together, 1, head_dim), lambda h: (first + h, 0, 0))]
        + [out_near] * 6,
        out_shape=[
            jax.ShapeDtypeStruct((tile_len, branches * head_dim), jnp.bfloat16),
            jax.ShapeDtypeStruct((branches, 1, head_dim), jnp.float32),
        ]
        + [part] * 6,
        input_output_aliases={13 + n: n for n in range(len(so_far))},
        scratch_shapes=[
            pltpu.VMEM((1, 9 * tile_len), jnp.float32),
            pltpu.VMEM((tile_len, 1), jnp.float32),
        ]
        + [
            pltpu.VMEM(score, jnp.float32),
            pltpu.VMEM(score, jnp.float32),
            pltpu.VMEM(score, jnp.bfloat16),
            pltpu.VMEM(score, jnp.bfloat16),
        ]
        * 2,
        compiler_params=pltpu.CompilerParams(vmem_limit_bytes=24 * 1024 * 1024),
        cost_estimate=pl.CostEstimate(
            flops=10 * pairs * head_dim,
            bytes_accessed=12 * 3 * tile_len * heads * head_dim * 2,
            transcendentals=pairs,
        ),
    )(*small, query, grad, *keys, *values, *so_far)


def pack_body(chunks, *refs):
    inputs, outputs = refs[:3], refs[3:]
    tile_len = inputs[0].shape[0]
    head_dim = inputs[0].shape[1] // sum(heads for _, heads in chunks)
    for (opening, heads), out_ref in zip(chunks, outputs):
        columns = slice(opening * head_dim, (opening + heads) * head_dim)
        for n in range(3):
            out_ref[n * tile_len : (n + 1) * tile_len] = inputs[n][:, columns]


def own_body(own_ref, out_ref):
    out_ref[...] = own_ref[...]


def packed(chunks, line):
    tile_len, width = line[0].shape
    whole = pl.BlockSpec(memory_space=pltpu.VMEM)
    own = pl.pallas_call(
        own_body,
        in_specs=[whole],
        out_specs=whole,
        out_shape=jax.ShapeDtypeStruct(line[0].shape, line[0].dtype),
        compiler_params=pltpu.CompilerParams(vmem_limit_bytes=8 * 1024 * 1024),
    )(line[0])
    line = (own,) + line[1:]
    per_head = width // sum(heads for _, heads in chunks)
    return pl.pallas_call(
        functools.partial(pack_body, chunks),
        in_specs=[whole] * 3,
        out_specs=[whole] * len(chunks),
        out_shape=[
            jax.ShapeDtypeStruct((3 * tile_len, heads * per_head), jnp.bfloat16)
            for _, heads in chunks
        ],
        compiler_params=pltpu.CompilerParams(vmem_limit_bytes=8 * 1024 * 1024),
    )(*line)


def on_device(
    probe_vectors,
    lookup_vectors,
    payload_vectors,
    result_derivative,
    patch_occupancy,
    patch_neighborhood_offset,
    sharpness,
):
    _, frames, high, cols, width = probe_vectors.shape
    tile_len = frames * high * cols
    branches = sharpness.shape[0]
    head_dim = width // branches

    def as_tokens(field):
        return jnp.transpose(field[0], (0, 2, 1, 3)).reshape(tile_len, width)

    def as_field(tokens):
        return jnp.transpose(tokens.reshape(frames, cols, high, width), (0, 2, 1, 3))[None]

    spot = np.arange(tile_len)
    slot = (spot // (cols * high) * high + spot % high) * cols + spot // high % cols
    slot_row = jnp.asarray(np.tile(slot, 9)[None, :], jnp.int32)
    slot_col = jnp.asarray(slot[:, None], jnp.int32)
    counts = patch_occupancy[0].T
    shifts = jnp.transpose(patch_neighborhood_offset[0], (1, 2, 0)).reshape(-1, counts.shape[1])
    small = (sharpness, counts, shifts, slot_row, slot_col)

    query, key, value, grad = (
        as_tokens(f) for f in (probe_vectors, lookup_vectors, payload_vectors, result_derivative)
    )
    chunks = ((0, 6), (6, 6))
    key_blocks = packed(chunks, (key, exchanged(key, "tm", 0), exchanged(key, "tm", 1)))
    value_blocks = packed(
        chunks, (value, exchanged(value, "height", 0), exchanged(value, "height", 1))
    )
    near = [
        (
            (keys, exchanged(keys, "height", 0), exchanged(keys, "height", 1)),
            (values, exchanged(values, "tm", 0), exchanged(values, "tm", 1)),
        )
        for keys, values in zip(key_blocks, value_blocks)
    ]
    results = ()
    for chunk, (keys, values) in zip(chunks, near):
        results = attention(
            chunk, branches, tile_len, head_dim, small, query, grad, keys, values, results
        )
    query_grad, sharpness_grad = results[0], results[1]

    def met(parts, axis):
        return parts[0], exchanged(parts[1], axis, 0), exchanged(parts[2], axis, 1)

    key_parts = met(results[2:5], "height")
    value_parts = met(results[5:8], "tm")
    wide, time_count = ("dp", "height"), lax.axis_size("tm")
    row = jnp.sum(sharpness_grad, axis=(1, 2))
    rows = jnp.broadcast_to(row, (math.prod(lax.axis_size(axis) for axis in wide), 1, branches))
    row, *summed = summed_parts(key_parts, swapped(rows, wide))
    (key_grad,) = final_sum(met(summed, "tm"))
    rows, *summed = summed_parts(value_parts, row, time_count)
    rows = swapped(rows, ("tm",))
    row, value_grad = final_sum(met(summed, "height"), rows)
    return as_field(query_grad), as_field(key_grad), as_field(value_grad), row[0]


def solution(mesh):
    field = P("dp", "tm", "height", None, None)
    return jax.shard_map(
        on_device,
        mesh=mesh,
        in_specs=(field,) * 4 + (P("dp", None, None), P("dp", None, None, None), P()),
        out_specs=(field,) * 3 + (P(),),
        check_vma=False,
    )
```

```python
import functools
import math

import jax
import jax.numpy as jnp
import numpy as np
from jax import lax
from jax.experimental import pallas as pl
from jax.experimental.pallas import tpu as pltpu
from jax.sharding import PartitionSpec as P

HIDDEN = -1e30


def exchanged(block, axis, turn):
    count = lax.axis_size(axis)
    partner = [(i + turn) // 2 * 4 + 1 - 2 * turn - i for i in range(count)]
    return lax.ppermute(block, axis, [(i, j) for i, j in enumerate(partner) if 0 <= j < count])


def swapped(rows, axes):
    return lax.all_to_all(rows, axes, 0, 0)


def sum_body(with_rows, *refs):
    if with_rows:
        rows_ref, row_ref = refs[0], refs[4]
        row_ref[...] = jnp.broadcast_to(jnp.sum(rows_ref[...], axis=0)[None], row_ref.shape)
        refs = refs[1:4] + refs[5:]
    own_ref, below_ref, above_ref, own_sum_ref, *side_refs = refs
    length = own_sum_ref.shape[0]
    for n in range(3):
        rows = slice(n * length, (n + 1) * length)
        summed = (
            own_ref[rows].astype(jnp.float32)
            + below_ref[rows].astype(jnp.float32)
            + above_ref[rows].astype(jnp.float32)
        )
        if n == 0:
            own_sum_ref[...] = summed
        else:
            side_refs[n - 1][...] = summed.astype(jnp.bfloat16)


def summed_parts(parts, rows=None, copies=1):
    tile = (parts[0].shape[0] // 3, parts[0].shape[1])
    vmem = pl.BlockSpec(memory_space=pltpu.VMEM)
    given = (() if rows is None else (rows,)) + tuple(parts)
    out_shape = [
        jax.ShapeDtypeStruct(tile, jnp.float32),
        jax.ShapeDtypeStruct(tile, jnp.bfloat16),
        jax.ShapeDtypeStruct(tile, jnp.bfloat16),
    ]
    if rows is not None:
        out_shape = [jax.ShapeDtypeStruct((copies,) + rows.shape[1:], jnp.float32)] + out_shape
    return pl.pallas_call(
        functools.partial(sum_body, rows is not None),
        in_specs=[vmem] * len(given),
        out_specs=[vmem] * len(out_shape),
        out_shape=out_shape,
        compiler_params=pltpu.CompilerParams(vmem_limit_bytes=16 * 1024 * 1024),
    )(*given)


def final_body(with_rows, *refs):
    if with_rows:
        rows_ref, row_ref = refs[0], refs[4]
        row_ref[...] = jnp.sum(rows_ref[...], axis=0)
        refs = refs[1:4] + refs[5:]
    own_ref, below_ref, above_ref, out_ref = refs
    out_ref[...] = (
        own_ref[...] + below_ref[...].astype(jnp.float32) + above_ref[...].astype(jnp.float32)
    ).astype(out_ref.dtype)


def final_sum(parts, rows=None):
    vmem = pl.BlockSpec(memory_space=pltpu.VMEM)
    given = (() if rows is None else (rows,)) + tuple(parts)
    out_shape = [jax.ShapeDtypeStruct(parts[0].shape, jnp.bfloat16)]
    if rows is not None:
        out_shape = [jax.ShapeDtypeStruct(rows.shape[1:], jnp.float32)] + out_shape
    return pl.pallas_call(
        functools.partial(final_body, rows is not None),
        in_specs=[vmem] * len(given),
        out_specs=[vmem] * len(out_shape),
        out_shape=out_shape,
        compiler_params=pltpu.CompilerParams(vmem_limit_bytes=8 * 1024 * 1024),
    )(*given)


KEY_SPOTS = [(a, b) for a in range(3) for b in range(3)]
VALUE_SPOTS = [(b, a) for a, b in KEY_SPOTS]


def line(place):
    first = 1 - 2 * (place % 2)
    return place, place + first, place - first


def raw_scores(query, grad, keys, values, logits_ref, grad_weight_ref):
    across = (((1,), (1,)), ((), ()))
    logits_ref[...] = lax.dot_general(query, keys, across, preferred_element_type=jnp.float32)
    grad_weight_ref[...] = lax.dot_general(
        grad, values, across, preferred_element_type=jnp.float32
    )


def score_gradients(multiplier, bias_ref, valid_ref, logits_ref, grad_weight_ref, low_ref, scaled_ref):
    rows_at_once = 48
    for first in range(0, logits_ref.shape[0], rows_at_once):
        rows = slice(first, first + rows_at_once)
        logits = logits_ref[rows] * multiplier + bias_ref[...]
        raised = jnp.exp2(logits - jnp.max(logits, axis=1, keepdims=True))
        total = jnp.sum(raised, axis=1, keepdims=True)
        weights = raised * (valid_ref[rows] / total)
        low = weights.astype(jnp.bfloat16)
        low_ref[rows] = low
        grad_weight = grad_weight_ref[rows]
        row_delta = jnp.sum(low.astype(jnp.float32) * grad_weight, axis=1, keepdims=True)
        scaled_ref[rows] = (weights * (grad_weight - row_delta)).astype(jnp.bfloat16)


def attention_body(
    opening,
    tile_len,
    together,
    kept,
    sharpness_ref,
    counts_ref,
    shifts_ref,
    slot_row_ref,
    slot_col_ref,
    query_ref,
    grad_ref,
    *refs,
):
    key_refs, value_refs = refs[:3], refs[3:6]
    refs = refs[6 + kept :]
    query_grad_ref, sharpness_grad_ref = refs[0], refs[1]
    key_part_refs, value_part_refs = refs[2:5], refs[5:8]
    bias_ref, valid_ref = refs[8], refs[9]
    work = (refs[10:14], refs[14:18])
    head_dim = query_ref.shape[1] // together
    time_tile = lax.axis_index("tm")
    high_tile = lax.axis_index("height")
    high_count, time_count = counts_ref.shape[0], counts_ref.shape[1]
    time_shift = shifts_ref[2 * high_tile, time_tile]
    high_shift = shifts_ref[2 * high_tile + 1, time_tile]

    @pl.when(pl.program_id(0) == 0)
    def _():
        limits = []
        times, highs = line(time_tile), line(high_tile)
        for a, b in KEY_SPOTS:
            t, h = times[b], highs[a]
            inside = (t >= 0) & (t < time_count) & (h >= 0) & (h < high_count)
            inside &= jnp.abs(t - time_tile - time_shift) <= 1
            inside &= jnp.abs(h - high_tile - high_shift) <= 1
            count = counts_ref[jnp.clip(h, 0, high_count - 1), jnp.clip(t, 0, time_count - 1)]
            limits.append(jnp.where(inside, count, 0))
        place = lax.broadcasted_iota(jnp.int32, slot_row_ref.shape, 1)
        limit_row = jnp.full(slot_row_ref.shape, limits[0], jnp.int32)
        for n in range(1, len(limits)):
            limit_row = jnp.where(place >= n * tile_len, limits[n], limit_row)
        bias_ref[...] = jnp.where(slot_row_ref[...] < limit_row, 0.0, HIDDEN)
        own_count = counts_ref[high_tile, time_tile]
        valid_ref[...] = jnp.where(slot_col_ref[...] < own_count, 1.0, 0.0)

    def tile(ref, n):
        return ref[n * tile_len : (n + 1) * tile_len]

    def operands(j):
        columns = slice(j * head_dim, (j + 1) * head_dim)
        place = (pl.program_id(0) * together + j) * head_dim
        near = pl.ds(pl.multiple_of(place, head_dim), head_dim)
        keys = jnp.concatenate([ref[:, near] for ref in key_refs], axis=0)
        values = jnp.concatenate(
            [value_refs[b][n * tile_len : (n + 1) * tile_len, near] for b, n in VALUE_SPOTS],
            axis=0,
        )
        return query_ref[:, columns], grad_ref[:, columns], keys, values

    def gradients(j):
        columns = slice(j * head_dim, (j + 1) * head_dim)
        query, grad, keys, values = operands(j)
        sharp = sharpness_ref[opening + pl.program_id(0) * together + j]
        factor = sharp * (1.0 / math.sqrt(head_dim))
        logits_ref, grad_weight_ref, low_ref, scaled_ref = work[j % 2]
        score_gradients(factor * math.log2(math.e), bias_ref, valid_ref, *work[j % 2])
        low, scaled = low_ref[...], scaled_ref[...]
        down = (((0,), (0,)), ((), ()))
        query_grad = jnp.dot(scaled, keys, preferred_element_type=jnp.float32) * factor
        query_grad_ref[:, columns] = query_grad.astype(jnp.bfloat16)
        sharpness_grad_ref[j] = jnp.sum(
            query_grad * query.astype(jnp.float32), axis=0, keepdims=True
        ) * (1.0 / sharp)
        part_key = lax.dot_general(scaled, query, down, preferred_element_type=jnp.float32)
        part_key = (part_key * factor).astype(jnp.bfloat16)
        part_value = lax.dot_general(low, grad, down, preferred_element_type=jnp.float32)
        part_value = part_value.astype(jnp.bfloat16)
        for n, ref in enumerate(key_part_refs):
            ref[:, columns] = part_key[3 * n * tile_len : 3 * (n + 1) * tile_len]
        for place, (b, n) in enumerate(VALUE_SPOTS):
            value_part_refs[b][n * tile_len : (n + 1) * tile_len, columns] = tile(
                part_value, place
            )

    raw_scores(*operands(0), *work[0][:2])
    for j in range(together):
        if j + 1 < together:
            raw_scores(*operands(j + 1), *work[(j + 1) % 2][:2])
        gradients(j)


def attention(chunk, branches, tile_len, head_dim, small, query, grad, keys, values, so_far):
    opening, heads = chunk
    together = heads
    first = opening // together
    smem = pl.BlockSpec(memory_space=pltpu.SMEM)
    whole = lambda array: pl.BlockSpec(array.shape, lambda h: (0, 0))
    side = pl.BlockSpec((tile_len, together * head_dim), lambda h: (0, first + h))
    out_near = pl.BlockSpec((3 * tile_len, together * head_dim), lambda h: (0, first + h))
    part = jax.ShapeDtypeStruct((3 * tile_len, branches * head_dim), jnp.bfloat16)
    pairs = heads * tile_len * 9 * tile_len
    score = (tile_len, 9 * tile_len)
    return pl.pallas_call(
        functools.partial(attention_body, opening, tile_len, together, len(so_far)),
        grid=(heads // together,),
        in_specs=[smem] * 3
        + [whole(small[3]), whole(small[4]), side, side]
        + [pl.BlockSpec(memory_space=pltpu.VMEM)] * 6
        + [pl.BlockSpec(memory_space=pl.ANY)] * len(so_far),
        out_specs=[side, pl.BlockSpec((together, 1, head_dim), lambda h: (first + h, 0, 0))]
        + [out_near] * 6,
        out_shape=[
            jax.ShapeDtypeStruct((tile_len, branches * head_dim), jnp.bfloat16),
            jax.ShapeDtypeStruct((branches, 1, head_dim), jnp.float32),
        ]
        + [part] * 6,
        input_output_aliases={13 + n: n for n in range(len(so_far))},
        scratch_shapes=[
            pltpu.VMEM((1, 9 * tile_len), jnp.float32),
            pltpu.VMEM((tile_len, 1), jnp.float32),
        ]
        + [
            pltpu.VMEM(score, jnp.float32),
            pltpu.VMEM(score, jnp.float32),
            pltpu.VMEM(score, jnp.bfloat16),
            pltpu.VMEM(score, jnp.bfloat16),
        ]
        * 2,
        compiler_params=pltpu.CompilerParams(vmem_limit_bytes=24 * 1024 * 1024),
        cost_estimate=pl.CostEstimate(
            flops=10 * pairs * head_dim,
            bytes_accessed=12 * 3 * tile_len * heads * head_dim * 2,
            transcendentals=pairs,
        ),
    )(*small, query, grad, *keys, *values, *so_far)


def pack_body(chunks, *refs):
    inputs, outputs = refs[:3], refs[3:]
    tile_len = inputs[0].shape[0]
    head_dim = inputs[0].shape[1] // sum(heads for _, heads in chunks)
    for (opening, heads), out_ref in zip(chunks, outputs):
        columns = slice(opening * head_dim, (opening + heads) * head_dim)
        for n in range(3):
            out_ref[n * tile_len : (n + 1) * tile_len] = inputs[n][:, columns]


def own_body(own_ref, out_ref):
    out_ref[...] = own_ref[...]


def packed(chunks, line):
    tile_len, width = line[0].shape
    whole = pl.BlockSpec(memory_space=pltpu.VMEM)
    own = pl.pallas_call(
        own_body,
        in_specs=[whole],
        out_specs=whole,
        out_shape=jax.ShapeDtypeStruct(line[0].shape, line[0].dtype),
        compiler_params=pltpu.CompilerParams(vmem_limit_bytes=8 * 1024 * 1024),
    )(line[0])
    line = (own,) + line[1:]
    per_head = width // sum(heads for _, heads in chunks)
    return pl.pallas_call(
        functools.partial(pack_body, chunks),
        in_specs=[whole] * 3,
        out_specs=[whole] * len(chunks),
        out_shape=[
            jax.ShapeDtypeStruct((3 * tile_len, heads * per_head), jnp.bfloat16)
            for _, heads in chunks
        ],
        compiler_params=pltpu.CompilerParams(vmem_limit_bytes=8 * 1024 * 1024),
    )(*line)


def on_device(
    probe_vectors,
    lookup_vectors,
    payload_vectors,
    result_derivative,
    patch_occupancy,
    patch_neighborhood_offset,
    sharpness,
):
    _, frames, high, cols, width = probe_vectors.shape
    tile_len = frames * high * cols
    branches = sharpness.shape[0]
    head_dim = width // branches

    def as_tokens(field):
        return jnp.transpose(field[0], (0, 2, 1, 3)).reshape(tile_len, width)

    def as_field(tokens):
        return jnp.transpose(tokens.reshape(frames, cols, high, width), (0, 2, 1, 3))[None]

    spot = np.arange(tile_len)
    slot = (spot // (cols * high) * high + spot % high) * cols + spot // high % cols
    slot_row = jnp.asarray(np.tile(slot, 9)[None, :], jnp.int32)
    slot_col = jnp.asarray(slot[:, None], jnp.int32)
    counts = patch_occupancy[0].T
    shifts = jnp.transpose(patch_neighborhood_offset[0], (1, 2, 0)).reshape(-1, counts.shape[1])
    small = (sharpness, counts, shifts, slot_row, slot_col)

    query, key, value, grad = (
        as_tokens(f) for f in (probe_vectors, lookup_vectors, payload_vectors, result_derivative)
    )
    chunks = ((0, 6), (6, 6))
    key_blocks = packed(chunks, (key, exchanged(key, "tm", 0), exchanged(key, "tm", 1)))
    value_blocks = packed(
        chunks, (value, exchanged(value, "height", 0), exchanged(value, "height", 1))
    )
    near = [
        (
            (keys, exchanged(keys, "height", 0), exchanged(keys, "height", 1)),
            (values, exchanged(values, "tm", 0), exchanged(values, "tm", 1)),
        )
        for keys, values in zip(key_blocks, value_blocks)
    ]
    results = ()
    for chunk, (keys, values) in zip(chunks, near):
        results = attention(
            chunk, branches, tile_len, head_dim, small, query, grad, keys, values, results
        )
    query_grad, sharpness_grad = results[0], results[1]

    def met(parts, axis):
        return parts[0], exchanged(parts[1], axis, 0), exchanged(parts[2], axis, 1)

    key_parts = met(results[2:5], "height")
    value_parts = met(results[5:8], "tm")
    wide, time_count = ("dp", "height"), lax.axis_size("tm")
    row = jnp.sum(sharpness_grad, axis=(1, 2))
    rows = jnp.broadcast_to(row, (math.prod(lax.axis_size(axis) for axis in wide), 1, branches))
    row, *summed = summed_parts(key_parts, swapped(rows, wide))
    (key_grad,) = final_sum(met(summed, "tm"))
    rows, *summed = summed_parts(value_parts, row, time_count)
    rows = swapped(rows, ("tm",))
    row, value_grad = final_sum(met(summed, "height"), rows)
    return as_field(query_grad), as_field(key_grad), as_field(value_grad), row[0]


def solution(mesh):
    field = P("dp", "tm", "height", None, None)
    return jax.shard_map(
        on_device,
        mesh=mesh,
        in_specs=(field,) * 4 + (P("dp", None, None), P("dp", None, None, None), P()),
        out_specs=(field,) * 3 + (P(),),
        check_vma=False,
    )
```
